32 devices in a mesh: dp: 8 (over y, x, core), tensor: 4 (over z).
Axes of the slice: x: 2, y: 2, z: 4, core: 2. Of those that a mesh axis runs over, the one named last changes fastest.
Arguments:
- queries: bfloat16 [2048, 8192], P('dp', 'tensor'), may hold values from -5 to 5
- keys_values: bfloat16 [2, 2048, 1024], P(None, 'dp', 'tensor'), may hold values from -5 to 5
- grad_out: bfloat16 [2048, 8192], P(('dp', 'tensor')), may hold values from -6 to 6
- piece_lengths: int32 [12], replicated, may hold values from 64 to 448, as said below
Outputs:
- grad_queries: bfloat16 [2048, 8192], P(('dp', 'tensor'))
- grad_keys_values: bfloat16 [2, 2048, 1024], P(None, 'dp', 'tensor')
The draws below stay inside these ranges and needn't reach their ends.
Inputs may be any that keep to these rules, and one draw needn't show every extreme that they name: `piece_lengths`: entry 3p (p < 4) is the length of prompt p, entries 3p + 1 and 3p + 2 the lengths of its chosen and rejected responses; the entries sum to 2048; a prompt with its two responses holds at most 36 * (32) rows.
All inputs are finite; a program needn't handle non-finite values.
Results may differ from the reference program's by a relative error of at most 0.028.
Values may be sent and summed in bfloat16 or wider, within the bound.
A program may use at most 128 MiB of HBM per device.

```python
import math
import jax
import jax.numpy as jnp
from jax import lax

HEADS = 64
KV_HEADS = 8
HEAD_DIM = 128
PROMPTS = 4
TOKENS = 2048


def draw_queries(key, part):
    key = jax.random.fold_in(key, 11)
    result = jnp.clip(jax.random.normal(key, (TOKENS, HEADS * HEAD_DIM), jnp.float32), -5.0, 5.0)
    return result.astype(jnp.bfloat16)


def draw_keys_values(key, part):
    key = jax.random.fold_in(key, 23)
    subkeys = jax.random.split(key, 2)
    keys = jnp.clip(jax.random.normal(subkeys[0], (TOKENS, KV_HEADS * HEAD_DIM), jnp.float32), -5.0, 5.0)
    values = jnp.clip(jax.random.normal(subkeys[1], (TOKENS, KV_HEADS * HEAD_DIM), jnp.float32), -5.0, 5.0)
    return jnp.stack([keys, values]).astype(jnp.bfloat16)


def draw_piece_lengths(key, part):
    key = jax.random.fold_in(key, 5)
    subkeys = jax.random.split(key, 3)
    unit_rows = TOKENS // 64
    other_prompts = jax.random.randint(subkeys[0], (2,), 4 * unit_rows, 6 * unit_rows + 1)
    spare = 12 * unit_rows - jnp.sum(other_prompts)
    steps_ids = jnp.arange(6, dtype=jnp.int32)
    extras = jnp.clip(spare - 2 * unit_rows * steps_ids, 0, 2 * unit_rows)
    extras = jax.random.permutation(subkeys[1], extras)
    replies = (2 * unit_rows + extras).reshape(3, 2)
    short_prompts = jnp.concatenate([jnp.array([4 * unit_rows], jnp.int32), other_prompts.astype(jnp.int32)])
    short_groups = jnp.concatenate([short_prompts[:, None], replies.astype(jnp.int32)], axis=1)
    long_group = jnp.array([[8 * unit_rows, 14 * unit_rows, 14 * unit_rows]], jnp.int32)
    groups = jnp.concatenate([long_group, short_groups], axis=0)
    order = jax.random.permutation(subkeys[2], PROMPTS)
    return groups[order].reshape(3 * PROMPTS).astype(jnp.int32)


def level_of(own_key, extent, cuts, low, largest):
    def one(dim, shards_of):
        steps = jax.random.uniform(jax.random.fold_in(jax.random.fold_in(own_key, 6), dim), (shards_of,), jnp.float32, low / len(cuts), largest / len(cuts))
        return jnp.repeat(jnp.exp(steps), extent[dim] // shards_of).reshape((-1,) + (1,) * (len(extent) - dim - 1))

    level = one(*cuts[0])
    for cut in cuts[1:]:
        level = level * one(*cut)
    return level


def normal_values(own_key, dims, width, reach, cuts=(), kind=jnp.bfloat16):
    factor_of = level_of(own_key, dims, cuts, -0.22, 0.18) if cuts else 1.0
    values = jax.random.normal(own_key, dims, jnp.float32) * width * factor_of
    return jnp.minimum(jnp.maximum(values, -reach), reach).astype(kind)


def setup_inputs(seed: int = 0) -> dict:
    key_of = jax.random.split(jax.random.key(seed), 5)
    return {
        "queries": draw_queries(jax.random.fold_in(key_of[4], 71), 0),
        "keys_values": draw_keys_values(jax.random.fold_in(key_of[4], 71), 0),
        "grad_out": normal_values(key_of[2], (TOKENS, HEADS * HEAD_DIM), 1.0, 6.0, ((0, 32),)),
        "piece_lengths": draw_piece_lengths(jax.random.fold_in(key_of[4], 71), 0),
    }


def piece_index(row_ids, piece_ends):
    return lax.optimization_barrier(jnp.sum((row_ids[:, None] >= piece_ends[None, :]).astype(jnp.int32), axis=1))

def visible(query_ids, query_piece, key_ids, key_piece):
    same_piece = key_piece[None, :] == query_piece[:, None]
    own_prompt = key_piece[None, :] == 3 * (query_piece[:, None] // 3)
    return (key_ids[None, :] <= query_ids[:, None]) & (same_piece | own_prompt)

def reference(queries, keys_values, grad_out, piece_lengths):
    group_size = HEADS // KV_HEADS
    inv_root = 1.0 / math.sqrt(HEAD_DIM)
    piece_ends = jnp.cumsum(piece_lengths).astype(jnp.int32)
    row_ids = jnp.arange(TOKENS, dtype=jnp.int32)
    pieces = piece_index(row_ids, piece_ends)
    allowed = visible(row_ids, pieces, row_ids, pieces)
    q_heads = queries.reshape(TOKENS, HEADS, HEAD_DIM).transpose(1, 0, 2)
    g_heads = grad_out.reshape(TOKENS, HEADS, HEAD_DIM).transpose(1, 0, 2)
    key_heads = keys_values[0].reshape(TOKENS, KV_HEADS, HEAD_DIM).transpose(1, 0, 2)
    value_heads = keys_values[1].reshape(TOKENS, KV_HEADS, HEAD_DIM).transpose(1, 0, 2)

    def one_head(head_index):
        kv_index = head_index // group_size
        query_rows = q_heads[head_index]
        grad_rows = g_heads[head_index]
        key_rows = key_heads[kv_index]
        value_rows = value_heads[kv_index]
        logits = jnp.dot(query_rows, key_rows.T, preferred_element_type=jnp.float32) * inv_root
        masked = jnp.where(allowed, logits, jnp.float32(-1e+30))
        row_top = lax.optimization_barrier(jnp.max(masked, axis=1))
        weights = jnp.where(allowed, jnp.exp(logits - row_top[:, None]), jnp.float32(0.0))
        attend = weights / lax.optimization_barrier(jnp.sum(weights, axis=1))[:, None]
        attend_low = attend.astype(jnp.bfloat16)
        outputs = jnp.dot(attend_low, value_rows, preferred_element_type=jnp.float32).astype(jnp.bfloat16)
        pushed = jnp.dot(grad_rows, value_rows.T, preferred_element_type=jnp.float32)
        row_delta = lax.optimization_barrier(jnp.sum(grad_rows.astype(jnp.float32) * outputs.astype(jnp.float32), axis=1))
        slopes = (attend * (pushed - row_delta[:, None])).astype(jnp.bfloat16)
        query_part = jnp.dot(slopes, key_rows, preferred_element_type=jnp.float32) * inv_root
        key_part = jnp.dot(slopes.T, query_rows, preferred_element_type=jnp.float32) * inv_root
        value_part = jnp.dot(attend_low.T, grad_rows, preferred_element_type=jnp.float32)
        return (query_part, key_part, value_part)
    query_part, key_part, value_part = lax.map(one_head, jnp.arange(HEADS, dtype=jnp.int32))
    grad_queries = query_part.transpose(1, 0, 2).reshape(TOKENS, HEADS * HEAD_DIM).astype(jnp.bfloat16)
    key_sum = key_part.reshape(KV_HEADS, group_size, TOKENS, HEAD_DIM).sum(axis=1)
    value_sum = value_part.reshape(KV_HEADS, group_size, TOKENS, HEAD_DIM).sum(axis=1)
    key_flat = key_sum.transpose(1, 0, 2).reshape(TOKENS, KV_HEADS * HEAD_DIM)
    value_flat = value_sum.transpose(1, 0, 2).reshape(TOKENS, KV_HEADS * HEAD_DIM)
    grad_keys_values = jnp.stack([key_flat, value_flat]).astype(jnp.bfloat16)
    return (grad_queries, grad_keys_values)
```

```python
import functools
import math

import jax
import jax.numpy as jnp
from jax import lax
from jax.experimental import pallas as pl
from jax.experimental.pallas import tpu as pltpu
from jax.sharding import PartitionSpec as P

HEAD_DIM = 128
GROUP = 8
PAIR = 2
MESH = pl.DeviceIdType.MESH
INV_ROOT = 1.0 / math.sqrt(HEAD_DIM)
EXP_SCALE = INV_ROOT * math.log2(math.e)


def dot(a, b):
    return jnp.dot(a, b, preferred_element_type=jnp.float32)


def dot_t(a, b):
    return lax.dot_general(a, b, (((1,), (1,)), ((), ())), preferred_element_type=jnp.float32)


def kernel(
    n_dp, n_t, back, len_ref, q_hbm, kv_hbm, go_hbm, gq_hbm, gkv_ref,
    q, g, dq, win, key_t, bias, prob, push, slope, acc, stage, own, recv,
    q_sem, kv_own_sem, g_own_sem, dq_own_sem,
    g_send, g_recv, kv_send, kv_recv, dq_send, dq_recv, dkv_send, dkv_recv,
):
    d = lax.axis_index("dp")
    t = lax.axis_index("tensor")
    rows, width = q.shape
    kv_heads = win.shape[0]
    blocks = back + 1
    slice_rows = go_hbm.shape[0]
    chunk_width = PAIR * HEAD_DIM
    chunks = width // chunk_width
    chunks_per_kv = GROUP // PAIR

    barrier = pltpu.get_barrier_semaphore()
    for step in range(1, n_dp):
        pl.semaphore_signal(barrier, inc=1, device_id=(lax.rem(d + step, n_dp), t), device_id_type=MESH)
    for step in range(1, n_t):
        pl.semaphore_signal(barrier, inc=1, device_id=(d, lax.rem(t + step, n_t)), device_id_type=MESH)

    def key_block(b):
        return pl.ds(b * rows, rows)

    q_copy = pltpu.make_async_copy(q_hbm, q, q_sem)
    q_copy.start()

    def kv_own_copy(c):
        return pltpu.make_async_copy(
            kv_hbm.at[:, :, pl.ds(c * HEAD_DIM, HEAD_DIM)],
            win.at[c, :, key_block(back), :],
            kv_own_sem.at[c],
        )

    for c in range(kv_heads):
        kv_own_copy(c).start()
    own_columns = pl.ds(pl.multiple_of(t * width, width), width)
    own_rows = pl.ds(pl.multiple_of(t * slice_rows, slice_rows), slice_rows)
    g_own_copy = pltpu.make_async_copy(go_hbm.at[:, own_columns], g.at[own_rows, :], g_own_sem)
    g_own_copy.start()

    pl.semaphore_wait(barrier, n_dp - 1 + n_t - 1)

    def kv_copy(c, step):
        return pltpu.make_async_remote_copy(
            src_ref=kv_hbm.at[:, :, pl.ds(c * HEAD_DIM, HEAD_DIM)],
            dst_ref=win.at[c, :, key_block(back - step), :],
            send_sem=kv_send.at[c, step - 1],
            recv_sem=kv_recv.at[c, step - 1],
            device_id=(lax.rem(d + step, n_dp), t),
            device_id_type=MESH,
        )

    def columns_of(holder, chunk):
        return pl.ds(pl.multiple_of(holder * width + chunk * chunk_width, chunk_width), chunk_width)

    def g_copy(chunk, step):
        target = lax.rem(t + step, n_t)
        return pltpu.make_async_remote_copy(
            src_ref=go_hbm.at[:, columns_of(target, chunk)],
            dst_ref=g.at[own_rows, columns_of(0, chunk)],
            send_sem=g_send.at[chunk, step - 1],
            recv_sem=g_recv.at[chunk, step - 1],
            device_id=(d, target),
            device_id_type=MESH,
        )

    def dq_copy(chunk, step):
        target = lax.rem(t + step, n_t)
        return pltpu.make_async_remote_copy(
            src_ref=dq.at[pl.ds(pl.multiple_of(target * slice_rows, slice_rows), slice_rows), columns_of(0, chunk)],
            dst_ref=gq_hbm.at[:, columns_of(t, chunk)],
            send_sem=dq_send.at[chunk, step - 1],
            recv_sem=dq_recv.at[chunk, step - 1],
            device_id=(d, target),
            device_id_type=MESH,
        )

    def dq_own_copy(chunk):
        return pltpu.make_async_copy(
            dq.at[own_rows, columns_of(0, chunk)], gq_hbm.at[:, columns_of(t, chunk)], dq_own_sem.at[chunk]
        )

    def dkv_copy(c, step):
        return pltpu.make_async_remote_copy(
            src_ref=stage.at[c, :, key_block(back - step), :],
            dst_ref=recv.at[c, step - 1],
            send_sem=dkv_send.at[c, step - 1],
            recv_sem=dkv_recv.at[c, step - 1],
            device_id=(lax.rem(d + n_dp - step, n_dp), t),
            device_id_type=MESH,
        )

    def send_kv(c):
        for step in range(1, blocks):
            @pl.when(d + step < n_dp)
            def _(step=step):
                kv_copy(c, step).start()

    send_kv(0)

    def send_g(chunk, carry):
        for step in range(1, n_t):
            g_copy(chunk, step).start()
        return carry

    lax.fori_loop(0, chunks, send_g, 0)
    for c in range(1, kv_heads):
        send_kv(c)

    for step in range(1, blocks):
        @pl.when(d < step)
        def _(step=step):
            win[:, :, key_block(back - step), :] = jnp.zeros((kv_heads, 2, rows, HEAD_DIM), jnp.bfloat16)

    pieces = len_ref.shape[0]
    ends = []
    total = jnp.int32(0)
    for piece in range(pieces):
        total = total + len_ref[piece]
        ends.append(total)
    query_ids = d * rows + lax.broadcasted_iota(jnp.int32, (8, rows), 1)
    query_piece = jnp.zeros((8, rows), jnp.int32)
    query_prompt = jnp.zeros((8, rows), jnp.int32)
    for piece in range(pieces):
        past = (query_ids >= ends[piece]).astype(jnp.int32)
        query_piece = query_piece + past
        if piece % 3 == 2:
            query_prompt = query_prompt + 3 * past
    query_ids, query_piece, query_prompt = query_ids[:1], query_piece[:1], query_prompt[:1]

    def mask_block(b, carry):
        key_ids = (d - back + b) * rows + lax.broadcasted_iota(jnp.int32, (rows, rows), 0)
        key_piece = jnp.zeros((rows, rows), jnp.int32)
        for piece in range(pieces):
            key_piece = key_piece + (key_ids >= ends[piece]).astype(jnp.int32)
        allowed = (key_ids <= query_ids) & (key_ids >= 0) & (
            (key_piece == query_piece) | (key_piece == query_prompt)
        )
        bias[pl.ds(pl.multiple_of(b * rows, rows), rows), :] = jnp.where(allowed, jnp.float32(0.0), jnp.float32(-1e30))
        return carry

    lax.fori_loop(0, blocks, mask_block, 0)
    q_copy.wait()
    g_own_copy.wait()

    def one_chunk(chunk, carry):
        c = chunk // chunks_per_kv
        place = lax.rem(chunk, chunks_per_kv)

        @pl.when(place == 0)
        def _():
            pltpu.make_async_copy(
                kv_hbm.at[:, :, pl.ds(0, HEAD_DIM)], win.at[c, :, key_block(back), :], kv_own_sem.at[c]
            ).wait()
            for step in range(1, blocks):
                @pl.when(d >= step)
                def _(step=step):
                    pltpu.make_async_remote_copy(
                        src_ref=kv_hbm.at[:, :, pl.ds(0, HEAD_DIM)],
                        dst_ref=win.at[c, :, key_block(back - step), :],
                        send_sem=kv_send.at[c, step - 1],
                        recv_sem=kv_recv.at[c, step - 1],
                        device_id=(lax.rem(d + step, n_dp), t),
                        device_id_type=MESH,
                    ).wait_recv()
            for b in range(blocks):
                key_t[:, key_block(b)] = win[c, 0, key_block(b), :].T
            acc[...] = jnp.zeros_like(acc)

        for step in range(1, n_t):
            g_copy(chunk, step).wait_recv()

        def heads_of(ref):
            return jnp.concatenate(
                [
                    ref[:, pl.ds(pl.multiple_of(chunk * chunk_width + u * HEAD_DIM, HEAD_DIM), HEAD_DIM)]
                    for u in range(PAIR)
                ],
                axis=0,
            )

        q_rows = heads_of(q)
        g_rows = heads_of(g)
        top = None
        for b in range(blocks):
            scores = dot_t(win[c, 0, key_block(b), :], q_rows)
            scores = scores + jnp.concatenate([bias[key_block(b), :]] * PAIR, axis=1)
            prob[key_block(b), :] = scores
            block_top = jnp.max(scores, axis=0, keepdims=True)
            top = block_top if top is None else jnp.maximum(top, block_top)
        weight_sum = jnp.zeros_like(top)
        push_sum = jnp.zeros_like(top)
        for b in range(blocks):
            weights = jnp.exp2((prob[key_block(b), :] - top) * EXP_SCALE)
            pushed = dot_t(win[c, 1, key_block(b), :], g_rows)
            prob[key_block(b), :] = weights
            push[key_block(b), :] = pushed
            weight_sum = weight_sum + jnp.sum(weights, axis=0, keepdims=True)
            push_sum = push_sum + jnp.sum(weights * pushed, axis=0, keepdims=True)
        inverse = 1.0 / weight_sum
        delta = push_sum * inverse
        for b in range(blocks):
            attend = prob[key_block(b), :] * inverse
            slopes = (attend * (push[key_block(b), :] - delta)).astype(jnp.bfloat16)
            slope[key_block(b), :] = slopes
            acc[0, key_block(b), :] += dot(slopes, q_rows)
            acc[1, key_block(b), :] += dot(attend.astype(jnp.bfloat16), g_rows)
        query_grad = dot(key_t[...], slope[...]) * INV_ROOT
        for u in range(PAIR):
            dq[:, pl.ds(pl.multiple_of(chunk * chunk_width + u * HEAD_DIM, HEAD_DIM), HEAD_DIM)] = (
                query_grad[:, u * rows : (u + 1) * rows].T.astype(jnp.bfloat16)
            )
        for step in range(1, n_t):
            dq_copy(chunk, step).start()
        dq_own_copy(chunk).start()

        @pl.when(place == chunks_per_kv - 1)
        def _():
            for b in range(blocks):
                key_part = acc[0, key_block(b), :] * INV_ROOT
                value_part = acc[1, key_block(b), :]
                if b == back:
                    own[c, 0] = key_part
                    own[c, 1] = value_part
                else:
                    stage[c, 0, key_block(b), :] = key_part.astype(jnp.bfloat16)
                    stage[c, 1, key_block(b), :] = value_part.astype(jnp.bfloat16)
            for step in range(1, blocks):
                @pl.when(d >= step)
                def _(step=step):
                    dkv_copy(c, step).start()

        return carry

    lax.fori_loop(0, chunks, one_chunk, 0)

    for c in range(kv_heads):
        for step in range(1, blocks):
            @pl.when(d + step < n_dp)
            def _(c=c, step=step):
                kv_copy(c, step).wait_send()
                dkv_copy(c, step).wait_recv()
                own[c] += recv[c, step - 1].astype(jnp.float32)
        gkv_ref[:, :, c * HEAD_DIM : (c + 1) * HEAD_DIM] = own[c].astype(jnp.bfloat16)
    for c in range(kv_heads):
        for step in range(1, blocks):
            @pl.when(d >= step)
            def _(c=c, step=step):
                dkv_copy(c, step).wait_send()

    def finish(chunk, carry):
        for step in range(1, n_t):
            g_copy(chunk, step).wait_send()
            dq_copy(chunk, step).wait()
        dq_own_copy(chunk).wait()
        return carry

    lax.fori_loop(0, chunks, finish, 0)


def body(n_dp, n_t, queries, keys_values, grad_out, piece_lengths):
    rows, width = queries.shape
    kv_heads = keys_values.shape[2] // HEAD_DIM
    tokens = rows * n_dp
    group_rows = 36 * (tokens // 64)
    back = min(n_dp - 1, -(-(group_rows - 1) // rows))
    keys = (back + 1) * rows
    chunks = width // (PAIR * HEAD_DIM)
    bf16, f32 = jnp.bfloat16, jnp.float32
    dma = pltpu.SemaphoreType.DMA
    lanes = PAIR * rows
    flops = 5 * 2 * rows * keys * width
    return pl.pallas_call(
        functools.partial(kernel, n_dp, n_t, back),
        out_shape=(
            jax.ShapeDtypeStruct(grad_out.shape, bf16),
            jax.ShapeDtypeStruct(keys_values.shape, bf16),
        ),
        in_specs=[
            pl.BlockSpec(memory_space=pltpu.SMEM),
            pl.BlockSpec(memory_space=pl.ANY),
            pl.BlockSpec(memory_space=pl.ANY),
            pl.BlockSpec(memory_space=pl.ANY),
        ],
        out_specs=(pl.BlockSpec(memory_space=pl.ANY), pl.BlockSpec(memory_space=pltpu.VMEM)),
        scratch_shapes=[
            pltpu.VMEM((rows, width), bf16),
            pltpu.VMEM((rows, width), bf16),
            pltpu.VMEM((rows, width), bf16),
            pltpu.VMEM((kv_heads, 2, keys, HEAD_DIM), bf16),
            pltpu.VMEM((HEAD_DIM, keys), bf16),
            pltpu.VMEM((keys, rows), f32),
            pltpu.VMEM((keys, lanes), f32),
            pltpu.VMEM((keys, lanes), f32),
            pltpu.VMEM((keys, lanes), bf16),
            pltpu.VMEM((2, keys, HEAD_DIM), f32),
            pltpu.VMEM((kv_heads, 2, keys, HEAD_DIM), bf16),
            pltpu.VMEM((kv_heads, 2, rows, HEAD_DIM), f32),
            pltpu.VMEM((kv_heads, back, 2, rows, HEAD_DIM), bf16),
            dma(()),
            dma((kv_heads,)),
            dma(()),
            dma((chunks,)),
            dma((chunks, n_t - 1)),
            dma((chunks, n_t - 1)),
            dma((kv_heads, back)),
            dma((kv_heads, back)),
            dma((chunks, n_t - 1)),
            dma((chunks, n_t - 1)),
            dma((kv_heads, back)),
            dma((kv_heads, back)),
        ],
        compiler_params=pltpu.CompilerParams(
            collective_id=0, has_side_effects=True, vmem_limit_bytes=56 * 1024 * 1024
        ),
        cost_estimate=pl.CostEstimate(flops=flops, bytes_accessed=8 * rows * width, transcendentals=0),
    )(piece_lengths, queries, keys_values, grad_out)


def solution(mesh):
    return jax.shard_map(
        functools.partial(body, mesh.shape["dp"], mesh.shape["tensor"]),
        mesh=mesh,
        in_specs=(P("dp", "tensor"), P(None, "dp", "tensor"), P(("dp", "tensor"), None), P()),
        out_specs=(P(("dp", "tensor"), None), P(None, "dp", "tensor")),
        check_vma=False,
    )
```

```python
import functools
import math

import jax
import jax.numpy as jnp
from jax import lax
from jax.experimental import pallas as pl
from jax.experimental.pallas import tpu as pltpu
from jax.sharding import PartitionSpec as P

HEAD_DIM = 128
GROUP = 8
PAIR = 2
MESH = pl.DeviceIdType.MESH
INV_ROOT = 1.0 / math.sqrt(HEAD_DIM)
EXP_SCALE = INV_ROOT * math.log2(math.e)


def dot(a, b):
    return jnp.dot(a, b, preferred_element_type=jnp.float32)


def dot_t(a, b):
    return lax.dot_general(a, b, (((1,), (1,)), ((), ())), preferred_element_type=jnp.float32)


def kernel(
    n_dp, n_t, back, len_ref, q_hbm, kv_hbm, go_hbm, gq_hbm, gkv_ref,
    q, g, dq, win, key_t, bias, prob, push, slope, acc, stage, own, recv, swap,
    q_sem, kv_own_sem, g_own_sem, dq_own_sem,
    g_send, g_recv, kv_send, kv_recv, dq_send, dq_recv, dkv_send, dkv_recv,
    pass_send, pass_recv, swap_send, swap_recv,
):
    d = lax.axis_index("dp")
    t = lax.axis_index("tensor")
    rows, width = q.shape
    kv_heads = win.shape[0]
    blocks = back + 1
    core = lax.rem(d, 2)
    partner = d + 1 - 2 * core
    full = (back - 1) // 2
    hops = [(j, 2 * j + 2) for j in range(full)] + [(full, 1), (full + 1, back)]

    def has_later(step):
        if step == 1:
            return core == 0
        return (d + step < n_dp) & ((core == 1) | (step % 2 == 0))

    def has_earlier(step):
        if step == 1:
            return core == 1
        return (d >= step) & ((core == 0) | (step % 2 == 0))
    slice_rows = go_hbm.shape[0]
    chunk_width = PAIR * HEAD_DIM
    chunks = width // chunk_width
    chunks_per_kv = GROUP // PAIR

    barrier = pltpu.get_barrier_semaphore()
    for step in range(1, n_dp):
        pl.semaphore_signal(barrier, inc=1, device_id=(lax.rem(d + step, n_dp), t), device_id_type=MESH)
    for step in range(1, n_t):
        pl.semaphore_signal(barrier, inc=1, device_id=(d, lax.rem(t + step, n_t)), device_id_type=MESH)

    def key_block(b):
        return pl.ds(b * rows, rows)

    q_copy = pltpu.make_async_copy(q_hbm, q, q_sem)
    q_copy.start()

    def kv_own_copy(c):
        return pltpu.make_async_copy(
            kv_hbm.at[:, :, pl.ds(c * HEAD_DIM, HEAD_DIM)],
            win.at[c, :, key_block(back), :],
            kv_own_sem.at[c],
        )

    for c in range(kv_heads):
        kv_own_copy(c).start()
    own_columns = pl.ds(pl.multiple_of(t * width, width), width)
    own_rows = pl.ds(pl.multiple_of(t * slice_rows, slice_rows), slice_rows)
    g_own_copy = pltpu.make_async_copy(go_hbm.at[:, own_columns], g.at[own_rows, :], g_own_sem)
    g_own_copy.start()

    pl.semaphore_wait(barrier, n_dp - 1 + n_t - 1)

    def dynamic_block(b):
        return pl.ds(pl.multiple_of(b * rows, rows), rows)

    def kv_copy(c, slot, step):
        return pltpu.make_async_remote_copy(
            src_ref=kv_hbm.at[:, :, pl.ds(c * HEAD_DIM, HEAD_DIM)],
            dst_ref=win.at[c, :, key_block(back - step), :],
            send_sem=kv_send.at[c, slot],
            recv_sem=kv_recv.at[c, slot],
            device_id=(lax.rem(d + step, n_dp), t),
            device_id_type=MESH,
        )

    def pass_copy(c, j):
        step = 2 * j + 2
        return pltpu.make_async_remote_copy(
            src_ref=win.at[c, :, key_block(back - step), :],
            dst_ref=win.at[c, :, dynamic_block(back - step - 1 + 2 * core), :],
            send_sem=pass_send.at[c, j],
            recv_sem=pass_recv.at[c, j],
            device_id=(partner, t),
            device_id_type=MESH,
        )

    def pass_arrival(c, j):
        step = 2 * j + 2
        return pltpu.make_async_remote_copy(
            src_ref=win.at[c, :, key_block(back - step), :],
            dst_ref=win.at[c, :, dynamic_block(back - step + 1 - 2 * core), :],
            send_sem=pass_send.at[c, j],
            recv_sem=pass_recv.at[c, j],
            device_id=(partner, t),
            device_id_type=MESH,
        )

    def pass_on(c):
        for j in range(full):
            @pl.when(has_earlier(2 * j + 2))
            def _(j=j):
                kv_copy(c, j, 2 * j + 2).wait_recv()
                pass_copy(c, j).start()

    def swap_copy(c, j):
        return pltpu.make_async_remote_copy(
            src_ref=stage.at[c, :, dynamic_block(back - 2 * j - 1 - 2 * core), :],
            dst_ref=swap.at[c, j],
            send_sem=swap_send.at[c, j],
            recv_sem=swap_recv.at[c, j],
            device_id=(partner, t),
            device_id_type=MESH,
        )

    def dkv_copy(c, slot, step):
        return pltpu.make_async_remote_copy(
            src_ref=stage.at[c, :, key_block(back - step), :],
            dst_ref=recv.at[c, slot],
            send_sem=dkv_send.at[c, slot],
            recv_sem=dkv_recv.at[c, slot],
            device_id=(lax.rem(d + n_dp - step, n_dp), t),
            device_id_type=MESH,
        )

    def send_sums(c):
        for j in range(full):
            @pl.when(has_earlier(2 * j + 2))
            def _(j=j):
                step = 2 * j + 2
                swap_copy(c, j).wait_recv()
                stage[c, :, key_block(back - step), :] = (
                    stage[c, :, key_block(back - step), :].astype(jnp.float32) + swap[c, j].astype(jnp.float32)
                ).astype(jnp.bfloat16)
                dkv_copy(c, j, step).start()

    def columns_of(holder, chunk):
        return pl.ds(pl.multiple_of(holder * width + chunk * chunk_width, chunk_width), chunk_width)

    def g_copy(chunk, step):
        target = lax.rem(t + step, n_t)
        return pltpu.make_async_remote_copy(
            src_ref=go_hbm.at[:, columns_of(target, chunk)],
            dst_ref=g.at[own_rows, columns_of(0, chunk)],
            send_sem=g_send.at[chunk, step - 1],
            recv_sem=g_recv.at[chunk, step - 1],
            device_id=(d, target),
            device_id_type=MESH,
        )

    def dq_copy(chunk, step):
        target = lax.rem(t + step, n_t)
        return pltpu.make_async_remote_copy(
            src_ref=dq.at[pl.ds(pl.multiple_of(target * slice_rows, slice_rows), slice_rows), columns_of(0, chunk)],
            dst_ref=gq_hbm.at[:, columns_of(t, chunk)],
            send_sem=dq_send.at[chunk, step - 1],
            recv_sem=dq_recv.at[chunk, step - 1],
            device_id=(d, target),
            device_id_type=MESH,
        )

    def dq_own_copy(chunk):
        return pltpu.make_async_copy(
            dq.at[own_rows, columns_of(0, chunk)], gq_hbm.at[:, columns_of(t, chunk)], dq_own_sem.at[chunk]
        )

    def send_kv(c):
        for slot, step in hops:
            @pl.when(has_later(step))
            def _(slot=slot, step=step):
                kv_copy(c, slot, step).start()

    send_kv(0)

    def send_g(chunk, carry):
        for step in range(1, n_t):
            g_copy(chunk, step).start()
        return carry

    lax.fori_loop(0, chunks, send_g, 0)
    for c in range(1, kv_heads):
        send_kv(c)

    for step in range(1, blocks):
        @pl.when(d < step)
        def _(step=step):
            win[:, :, key_block(back - step), :] = jnp.zeros((kv_heads, 2, rows, HEAD_DIM), jnp.bfloat16)

    pieces = len_ref.shape[0]
    ends = []
    total = jnp.int32(0)
    for piece in range(pieces):
        total = total + len_ref[piece]
        ends.append(total)
    query_ids = d * rows + lax.broadcasted_iota(jnp.int32, (8, rows), 1)
    query_piece = jnp.zeros((8, rows), jnp.int32)
    query_prompt = jnp.zeros((8, rows), jnp.int32)
    for piece in range(pieces):
        past = (query_ids >= ends[piece]).astype(jnp.int32)
        query_piece = query_piece + past
        if piece % 3 == 2:
            query_prompt = query_prompt + 3 * past
    query_ids, query_piece, query_prompt = query_ids[:1], query_piece[:1], query_prompt[:1]

    def mask_block(b, carry):
        key_ids = (d - back + b) * rows + lax.broadcasted_iota(jnp.int32, (rows, rows), 0)
        key_piece = jnp.zeros((rows, rows), jnp.int32)
        for piece in range(pieces):
            key_piece = key_piece + (key_ids >= ends[piece]).astype(jnp.int32)
        allowed = (key_ids <= query_ids) & (key_ids >= 0) & (
            (key_piece == query_piece) | (key_piece == query_prompt)
        )
        bias[pl.ds(pl.multiple_of(b * rows, rows), rows), :] = jnp.where(allowed, jnp.float32(0.0), jnp.float32(-1e30))
        return carry

    lax.fori_loop(0, blocks, mask_block, 0)
    q_copy.wait()
    g_own_copy.wait()
    pass_on(0)

    def one_chunk(chunk, carry):
        c = chunk // chunks_per_kv
        place = lax.rem(chunk, chunks_per_kv)

        @pl.when(place == 0)
        def _():
            pltpu.make_async_copy(
                kv_hbm.at[:, :, pl.ds(0, HEAD_DIM)], win.at[c, :, key_block(back), :], kv_own_sem.at[c]
            ).wait()
            for slot, step in hops[full:]:
                @pl.when(has_earlier(step))
                def _(slot=slot, step=step):
                    pltpu.make_async_remote_copy(
                        src_ref=kv_hbm.at[:, :, pl.ds(0, HEAD_DIM)],
                        dst_ref=win.at[c, :, key_block(back - step), :],
                        send_sem=kv_send.at[c, slot],
                        recv_sem=kv_recv.at[c, slot],
                        device_id=(lax.rem(d + step, n_dp), t),
                        device_id_type=MESH,
                    ).wait_recv()
            for j in range(full):
                @pl.when(has_earlier(2 * j + 2))
                def _(j=j):
                    pass_arrival(c, j).wait_recv()
            for b in range(blocks):
                key_t[:, key_block(b)] = win[c, 0, key_block(b), :].T
            acc[...] = jnp.zeros_like(acc)

        for step in range(1, n_t):
            g_copy(chunk, step).wait_recv()

        def heads_of(ref):
            return jnp.concatenate(
                [
                    ref[:, pl.ds(pl.multiple_of(chunk * chunk_width + u * HEAD_DIM, HEAD_DIM), HEAD_DIM)]
                    for u in range(PAIR)
                ],
                axis=0,
            )

        q_rows = heads_of(q)
        g_rows = heads_of(g)
        top = None
        for b in range(blocks):
            scores = dot_t(win[c, 0, key_block(b), :], q_rows)
            scores = scores + jnp.concatenate([bias[key_block(b), :]] * PAIR, axis=1)
            prob[key_block(b), :] = scores
            block_top = jnp.max(scores, axis=0, keepdims=True)
            top = block_top if top is None else jnp.maximum(top, block_top)
        weight_sum = jnp.zeros_like(top)
        push_sum = jnp.zeros_like(top)
        for b in range(blocks):
            weights = jnp.exp2((prob[key_block(b), :] - top) * EXP_SCALE)
            pushed = dot_t(win[c, 1, key_block(b), :], g_rows)
            prob[key_block(b), :] = weights
            push[key_block(b), :] = pushed
            weight_sum = weight_sum + jnp.sum(weights, axis=0, keepdims=True)
            push_sum = push_sum + jnp.sum(weights * pushed, axis=0, keepdims=True)
        inverse = 1.0 / weight_sum
        delta = push_sum * inverse
        for b in range(blocks):
            attend = prob[key_block(b), :] * inverse
            slopes = (attend * (push[key_block(b), :] - delta)).astype(jnp.bfloat16)
            slope[key_block(b), :] = slopes
            acc[0, key_block(b), :] += dot(slopes, q_rows)
            acc[1, key_block(b), :] += dot(attend.astype(jnp.bfloat16), g_rows)
        query_grad = dot(key_t[...], slope[...]) * INV_ROOT
        for u in range(PAIR):
            dq[:, pl.ds(pl.multiple_of(chunk * chunk_width + u * HEAD_DIM, HEAD_DIM), HEAD_DIM)] = (
                query_grad[:, u * rows : (u + 1) * rows].T.astype(jnp.bfloat16)
            )
        for step in range(1, n_t):
            dq_copy(chunk, step).start()
        dq_own_copy(chunk).start()

        @pl.when(place == chunks_per_kv - 1)
        def _():
            for b in range(blocks):
                key_part = acc[0, key_block(b), :] * INV_ROOT
                value_part = acc[1, key_block(b), :]
                if b == back:
                    own[c, 0] = key_part
                    own[c, 1] = value_part
                else:
                    stage[c, 0, key_block(b), :] = key_part.astype(jnp.bfloat16)
                    stage[c, 1, key_block(b), :] = value_part.astype(jnp.bfloat16)
            for j in range(full):
                @pl.when(has_earlier(2 * j + 2))
                def _(j=j):
                    swap_copy(c, j).start()
            for slot, step in hops[full:]:
                @pl.when(has_earlier(step))
                def _(slot=slot, step=step):
                    dkv_copy(c, slot, step).start()

        for later in range(1, kv_heads):
            @pl.when(chunk == (later - 1) * chunks_per_kv + 1)
            def _(later=later):
                pass_on(later)

            @pl.when(chunk == later * chunks_per_kv)
            def _(later=later):
                send_sums(later - 1)

        return carry

    lax.fori_loop(0, chunks, one_chunk, 0)
    send_sums(kv_heads - 1)

    for c in range(kv_heads):
        for slot, step in hops:
            @pl.when(has_later(step))
            def _(c=c, slot=slot, step=step):
                kv_copy(c, slot, step).wait_send()
                dkv_copy(c, slot, step).wait_recv()
                own[c] += recv[c, slot].astype(jnp.float32)
        gkv_ref[:, :, c * HEAD_DIM : (c + 1) * HEAD_DIM] = own[c].astype(jnp.bfloat16)
    for c in range(kv_heads):
        for slot, step in hops:
            @pl.when(has_earlier(step))
            def _(c=c, slot=slot, step=step):
                dkv_copy(c, slot, step).wait_send()
        for j in range(full):
            @pl.when(has_earlier(2 * j + 2))
            def _(c=c, j=j):
                pass_copy(c, j).wait_send()
                swap_copy(c, j).wait_send()

    def finish(chunk, carry):
        for step in range(1, n_t):
            g_copy(chunk, step).wait_send()
            dq_copy(chunk, step).wait()
        dq_own_copy(chunk).wait()
        return carry

    lax.fori_loop(0, chunks, finish, 0)


def hand_over(query_grad, key_grad):
    slice_rows, width = query_grad.shape
    slabs = slice_rows // 16
    halves = 2

    def move(a, b, a_out, b_out, sems):
        copies = [pltpu.make_async_copy(b, b_out, sems.at[slabs * halves])]
        for i in range(slabs):
            for half in range(halves):
                part = (pl.ds(i * 16, 16), pl.ds(half * (width // halves), width // halves))
                copies.append(pltpu.make_async_copy(a.at[part], a_out.at[part], sems.at[i * halves + half]))
        for copy in copies:
            copy.start()
        for copy in copies:
            copy.wait()

    return pl.pallas_call(
        move,
        out_shape=(
            jax.ShapeDtypeStruct(query_grad.shape, query_grad.dtype),
            jax.ShapeDtypeStruct(key_grad.shape, key_grad.dtype),
        ),
        in_specs=[pl.BlockSpec(memory_space=pl.ANY)] * 2,
        out_specs=(pl.BlockSpec(memory_space=pl.ANY), pl.BlockSpec(memory_space=pl.ANY)),
        scratch_shapes=[pltpu.SemaphoreType.DMA((slabs * halves + 1,))],
    )(query_grad, key_grad)


def body(n_dp, n_t, queries, keys_values, grad_out, piece_lengths):
    rows, width = queries.shape
    kv_heads = keys_values.shape[2] // HEAD_DIM
    tokens = rows * n_dp
    group_rows = 36 * (tokens // 64)
    back = min(n_dp - 1, -(-(group_rows - 1) // rows) // 2 * 2 + 1)
    full = (back - 1) // 2
    keys = (back + 1) * rows
    chunks = width // (PAIR * HEAD_DIM)
    bf16, f32 = jnp.bfloat16, jnp.float32
    dma = pltpu.SemaphoreType.DMA
    lanes = PAIR * rows
    flops = 5 * 2 * rows * keys * width
    results = pl.pallas_call(
        functools.partial(kernel, n_dp, n_t, back),
        out_shape=(
            jax.ShapeDtypeStruct(grad_out.shape, bf16),
            jax.ShapeDtypeStruct(keys_values.shape, bf16),
        ),
        in_specs=[
            pl.BlockSpec(memory_space=pltpu.SMEM),
            pl.BlockSpec(memory_space=pl.ANY),
            pl.BlockSpec(memory_space=pl.ANY),
            pl.BlockSpec(memory_space=pl.ANY),
        ],
        out_specs=(pl.BlockSpec(memory_space=pl.ANY), pl.BlockSpec(memory_space=pltpu.VMEM)),
        scratch_shapes=[
            pltpu.VMEM((rows, width), bf16),
            pltpu.VMEM((rows, width), bf16),
            pltpu.VMEM((rows, width), bf16),
            pltpu.VMEM((kv_heads, 2, keys, HEAD_DIM), bf16),
            pltpu.VMEM((HEAD_DIM, keys), bf16),
            pltpu.VMEM((keys, rows), f32),
            pltpu.VMEM((keys, lanes), f32),
            pltpu.VMEM((keys, lanes), f32),
            pltpu.VMEM((keys, lanes), bf16),
            pltpu.VMEM((2, keys, HEAD_DIM), f32),
            pltpu.VMEM((kv_heads, 2, keys, HEAD_DIM), bf16),
            pltpu.VMEM((kv_heads, 2, rows, HEAD_DIM), f32),
            pltpu.VMEM((kv_heads, full + 2, 2, rows, HEAD_DIM), bf16),
            pltpu.VMEM((kv_heads, full, 2, rows, HEAD_DIM), bf16),
            dma(()),
            dma((kv_heads,)),
            dma(()),
            dma((chunks,)),
            dma((chunks, n_t - 1)),
            dma((chunks, n_t - 1)),
            dma((kv_heads, full + 2)),
            dma((kv_heads, full + 2)),
            dma((chunks, n_t - 1)),
            dma((chunks, n_t - 1)),
            dma((kv_heads, full + 2)),
            dma((kv_heads, full + 2)),
            dma((kv_heads, full)),
            dma((kv_heads, full)),
            dma((kv_heads, full)),
            dma((kv_heads, full)),
        ],
        compiler_params=pltpu.CompilerParams(
            collective_id=0, has_side_effects=True, vmem_limit_bytes=56 * 1024 * 1024
        ),
        cost_estimate=pl.CostEstimate(flops=flops, bytes_accessed=8 * rows * width, transcendentals=0),
    )(piece_lengths, queries, keys_values, grad_out)
    return hand_over(*results)


def solution(mesh):
    return jax.shard_map(
        functools.partial(body, mesh.shape["dp"], mesh.shape["tensor"]),
        mesh=mesh,
        in_specs=(P("dp", "tensor"), P(None, "dp", "tensor"), P(("dp", "tensor"), None), P()),
        out_specs=(P(("dp", "tensor"), None), P(None, "dp", "tensor")),
        check_vma=False,
    )
```

```python
import functools
import math

import jax
import jax.numpy as jnp
from jax import lax
from jax.experimental import pallas as pl
from jax.experimental.pallas import tpu as pltpu
from jax.sharding import PartitionSpec as P

HEAD_DIM = 128
GROUP = 8
PAIR = 2
MESH = pl.DeviceIdType.MESH
INV_ROOT = 1.0 / math.sqrt(HEAD_DIM)
EXP_SCALE = INV_ROOT * math.log2(math.e)


def dot(a, b):
    return jnp.dot(a, b, preferred_element_type=jnp.float32)


def dot_t(a, b):
    return lax.dot_general(a, b, (((1,), (1,)), ((), ())), preferred_element_type=jnp.float32)


def kernel(
    n_dp, n_t, back, len_ref, q_hbm, kv_hbm, go_hbm, gq_hbm, gkv_ref,
    q, g, dq, win, key_t, bias, prob, push, slope, acc, stage, own, recv, swap,
    q_sem, kv_own_sem, g_own_sem, dq_own_sem,
    g_send, g_recv, kv_send, kv_recv, dq_send, dq_recv, dkv_send, dkv_recv,
    pass_send, pass_recv, swap_send, swap_recv,
):
    d = lax.axis_index("dp")
    t = lax.axis_index("tensor")
    rows, width = q.shape
    kv_heads = win.shape[0]
    blocks = back + 1
    core = lax.rem(d, 2)
    partner = d + 1 - 2 * core
    full = (back - 1) // 2
    hops = [(j, 2 * j + 2) for j in range(full)] + [(full, 1), (full + 1, back)]

    def has_later(step):
        if step == 1:
            return core == 0
        return (d + step < n_dp) & ((core == 1) | (step % 2 == 0))

    def has_earlier(step):
        if step == 1:
            return core == 1
        return (d >= step) & ((core == 0) | (step % 2 == 0))
    slice_rows = go_hbm.shape[0]
    chunk_width = PAIR * HEAD_DIM
    chunks = width // chunk_width
    chunks_per_kv = GROUP // PAIR

    barrier = pltpu.get_barrier_semaphore()
    for step in range(1, n_dp):
        pl.semaphore_signal(barrier, inc=1, device_id=(lax.rem(d + step, n_dp), t), device_id_type=MESH)
    for step in range(1, n_t):
        pl.semaphore_signal(barrier, inc=1, device_id=(d, lax.rem(t + step, n_t)), device_id_type=MESH)

    def key_block(b):
        return pl.ds(b * rows, rows)

    q_copy = pltpu.make_async_copy(q_hbm, q, q_sem)
    q_copy.start()

    def kv_own_copy(c):
        return pltpu.make_async_copy(
            kv_hbm.at[:, :, pl.ds(c * HEAD_DIM, HEAD_DIM)],
            win.at[c, :, key_block(back), :],
            kv_own_sem.at[c],
        )

    for c in range(kv_heads):
        kv_own_copy(c).start()
    own_columns = pl.ds(pl.multiple_of(t * width, width), width)
    own_rows = pl.ds(pl.multiple_of(t * slice_rows, slice_rows), slice_rows)
    g_own_copy = pltpu.make_async_copy(go_hbm.at[:, own_columns], g.at[own_rows, :], g_own_sem)
    g_own_copy.start()

    pl.semaphore_wait(barrier, n_dp - 1 + n_t - 1)

    def dynamic_block(b):
        return pl.ds(pl.multiple_of(b * rows, rows), rows)

    def kv_copy(c, slot, step):
        return pltpu.make_async_remote_copy(
            src_ref=kv_hbm.at[:, :, pl.ds(c * HEAD_DIM, HEAD_DIM)],
            dst_ref=win.at[c, :, key_block(back - step), :],
            send_sem=kv_send.at[c, slot],
            recv_sem=kv_recv.at[c, slot],
            device_id=(lax.rem(d + step, n_dp), t),
            device_id_type=MESH,
        )

    def pass_copy(c, j):
        step = 2 * j + 2
        return pltpu.make_async_remote_copy(
            src_ref=win.at[c, :, key_block(back - step), :],
            dst_ref=win.at[c, :, dynamic_block(back - step - 1 + 2 * core), :],
            send_sem=pass_send.at[c, j],
            recv_sem=pass_recv.at[c, j],
            device_id=(partner, t),
            device_id_type=MESH,
        )

    def pass_arrival(c, j):
        step = 2 * j + 2
        return pltpu.make_async_remote_copy(
            src_ref=win.at[c, :, key_block(back - step), :],
            dst_ref=win.at[c, :, dynamic_block(back - step + 1 - 2 * core), :],
            send_sem=pass_send.at[c, j],
            recv_sem=pass_recv.at[c, j],
            device_id=(partner, t),
            device_id_type=MESH,
        )

    def pass_on(c):
        for j in range(full):
            @pl.when(has_earlier(2 * j + 2))
            def _(j=j):
                kv_copy(c, j, 2 * j + 2).wait_recv()
                pass_copy(c, j).start()

    def swap_copy(c, j):
        return pltpu.make_async_remote_copy(
            src_ref=stage.at[c, :, dynamic_block(back - 2 * j - 1 - 2 * core), :],
            dst_ref=swap.at[c, j],
            send_sem=swap_send.at[c, j],
            recv_sem=swap_recv.at[c, j],
            device_id=(partner, t),
            device_id_type=MESH,
        )

    def dkv_copy(c, slot, step):
        return pltpu.make_async_remote_copy(
            src_ref=stage.at[c, :, key_block(back - step), :],
            dst_ref=recv.at[c, slot],
            send_sem=dkv_send.at[c, slot],
            recv_sem=dkv_recv.at[c, slot],
            device_id=(lax.rem(d + n_dp - step, n_dp), t),
            device_id_type=MESH,
        )

    def send_sums(c):
        for j in range(full):
            @pl.when(has_earlier(2 * j + 2))
            def _(j=j):
                step = 2 * j + 2
                swap_copy(c, j).wait_recv()
                stage[c, :, key_block(back - step), :] = (
                    stage[c, :, key_block(back - step), :].astype(jnp.float32) + swap[c, j].astype(jnp.float32)
                ).astype(jnp.bfloat16)
                dkv_copy(c, j, step).start()

    def columns_of(holder, chunk):
        return pl.ds(pl.multiple_of(holder * width + chunk * chunk_width, chunk_width), chunk_width)

    def g_copy(chunk, step):
        target = lax.rem(t + step, n_t)
        return pltpu.make_async_remote_copy(
            src_ref=go_hbm.at[:, columns_of(target, chunk)],
            dst_ref=g.at[own_rows, columns_of(0, chunk)],
            send_sem=g_send.at[chunk, step - 1],
            recv_sem=g_recv.at[chunk, step - 1],
            device_id=(d, target),
            device_id_type=MESH,
        )

    def dq_copy(chunk, step):
        target = lax.rem(t + step, n_t)
        return pltpu.make_async_remote_copy(
            src_ref=dq.at[pl.ds(pl.multiple_of(target * slice_rows, slice_rows), slice_rows), columns_of(0, chunk)],
            dst_ref=gq_hbm.at[:, columns_of(t, chunk)],
            send_sem=dq_send.at[chunk, step - 1],
            recv_sem=dq_recv.at[chunk, step - 1],
            device_id=(d, target),
            device_id_type=MESH,
        )

    def dq_own_copy(chunk):
        return pltpu.make_async_copy(
            dq.at[own_rows, columns_of(0, chunk)], gq_hbm.at[:, columns_of(t, chunk)], dq_own_sem.at[chunk]
        )

    def send_kv(c):
        for slot, step in hops:
            @pl.when(has_later(step))
            def _(slot=slot, step=step):
                kv_copy(c, slot, step).start()

    send_kv(0)

    def send_g(chunk, carry):
        for step in range(1, n_t):
            g_copy(chunk, step).start()
        return carry

    lax.fori_loop(0, chunks, send_g, 0)
    for c in range(1, kv_heads):
        send_kv(c)

    for step in range(1, blocks):
        @pl.when(d < step)
        def _(step=step):
            win[:, :, key_block(back - step), :] = jnp.zeros((kv_heads, 2, rows, HEAD_DIM), jnp.bfloat16)

    pieces = len_ref.shape[0]
    ends = []
    total = jnp.int32(0)
    for piece in range(pieces):
        total = total + len_ref[piece]
        ends.append(total)
    query_ids = d * rows + lax.broadcasted_iota(jnp.int32, (8, rows), 1)
    query_piece = jnp.zeros((8, rows), jnp.int32)
    query_prompt = jnp.zeros((8, rows), jnp.int32)
    for piece in range(pieces):
        past = (query_ids >= ends[piece]).astype(jnp.int32)
        query_piece = query_piece + past
        if piece % 3 == 2:
            query_prompt = query_prompt + 3 * past
    query_ids, query_piece, query_prompt = query_ids[:1], query_piece[:1], query_prompt[:1]

    def mask_block(b, carry):
        key_ids = (d - back + b) * rows + lax.broadcasted_iota(jnp.int32, (rows, rows), 0)
        key_piece = jnp.zeros((rows, rows), jnp.int32)
        for piece in range(pieces):
            key_piece = key_piece + (key_ids >= ends[piece]).astype(jnp.int32)
        allowed = (key_ids <= query_ids) & (key_ids >= 0) & (
            (key_piece == query_piece) | (key_piece == query_prompt)
        )
        bias[pl.ds(pl.multiple_of(b * rows, rows), rows), :] = jnp.where(allowed, jnp.float32(0.0), jnp.float32(-1e30))
        return carry

    lax.fori_loop(0, blocks, mask_block, 0)
    q_copy.wait()
    g_own_copy.wait()
    pass_on(0)

    def one_chunk(chunk, carry):
        c = chunk // chunks_per_kv
        place = lax.rem(chunk, chunks_per_kv)

        @pl.when(place == 0)
        def _():
            pltpu.make_async_copy(
                kv_hbm.at[:, :, pl.ds(0, HEAD_DIM)], win.at[c, :, key_block(back), :], kv_own_sem.at[c]
            ).wait()
            for slot, step in hops[full:]:
                @pl.when(has_earlier(step))
                def _(slot=slot, step=step):
                    pltpu.make_async_remote_copy(
                        src_ref=kv_hbm.at[:, :, pl.ds(0, HEAD_DIM)],
                        dst_ref=win.at[c, :, key_block(back - step), :],
                        send_sem=kv_send.at[c, slot],
                        recv_sem=kv_recv.at[c, slot],
                        device_id=(lax.rem(d + step, n_dp), t),
                        device_id_type=MESH,
                    ).wait_recv()
            for j in range(full):
                @pl.when(has_earlier(2 * j + 2))
                def _(j=j):
                    pass_arrival(c, j).wait_recv()
            for b in range(blocks):
                key_t[:, key_block(b)] = win[c, 0, key_block(b), :].T
            acc[...] = jnp.zeros_like(acc)

        for step in range(1, n_t):
            g_copy(chunk, step).wait_recv()

        def heads_of(ref):
            return jnp.concatenate(
                [
                    ref[:, pl.ds(pl.multiple_of(chunk * chunk_width + u * HEAD_DIM, HEAD_DIM), HEAD_DIM)]
                    for u in range(PAIR)
                ],
                axis=0,
            )

        q_rows = heads_of(q)
        g_rows = heads_of(g)
        top = None
        for b in range(blocks):
            scores = dot_t(win[c, 0, key_block(b), :], q_rows)
            scores = scores + jnp.concatenate([bias[key_block(b), :]] * PAIR, axis=1)
            prob[key_block(b), :] = scores
            block_top = jnp.max(scores, axis=0, keepdims=True)
            top = block_top if top is None else jnp.maximum(top, block_top)
        weight_sum = jnp.zeros_like(top)
        push_sum = jnp.zeros_like(top)
        for b in range(blocks):
            weights = jnp.exp2((prob[key_block(b), :] - top) * EXP_SCALE)
            pushed = dot_t(win[c, 1, key_block(b), :], g_rows)
            prob[key_block(b), :] = weights
            push[key_block(b), :] = pushed
            weight_sum = weight_sum + jnp.sum(weights, axis=0, keepdims=True)
            push_sum = push_sum + jnp.sum(weights * pushed, axis=0, keepdims=True)
        inverse = 1.0 / weight_sum
        delta = push_sum * inverse
        for b in range(blocks):
            attend = prob[key_block(b), :] * inverse
            slopes = (attend * (push[key_block(b), :] - delta)).astype(jnp.bfloat16)
            slope[key_block(b), :] = slopes
            acc[0, key_block(b), :] += dot(slopes, q_rows)
            acc[1, key_block(b), :] += dot(attend.astype(jnp.bfloat16), g_rows)
        query_grad = dot(key_t[...], slope[...]) * INV_ROOT
        for u in range(PAIR):
            dq[:, pl.ds(pl.multiple_of(chunk * chunk_width + u * HEAD_DIM, HEAD_DIM), HEAD_DIM)] = (
                query_grad[:, u * rows : (u + 1) * rows].T.astype(jnp.bfloat16)
            )
        for step in range(1, n_t):
            dq_copy(chunk, step).start()
        dq_own_copy(chunk).start()

        @pl.when(place == chunks_per_kv - 1)
        def _():
            for b in range(blocks):
                key_part = acc[0, key_block(b), :] * INV_ROOT
                value_part = acc[1, key_block(b), :]
                if b == back:
                    own[c, 0] = key_part
                    own[c, 1] = value_part
                else:
                    stage[c, 0, key_block(b), :] = key_part.astype(jnp.bfloat16)
                    stage[c, 1, key_block(b), :] = value_part.astype(jnp.bfloat16)
            for j in range(full):
                @pl.when(has_earlier(2 * j + 2))
                def _(j=j):
                    swap_copy(c, j).start()
            for slot, step in hops[full:]:
                @pl.when(has_earlier(step))
                def _(slot=slot, step=step):
                    dkv_copy(c, slot, step).start()

        for later in range(1, kv_heads):
            @pl.when(chunk == (later - 1) * chunks_per_kv + 1)
            def _(later=later):
                pass_on(later)

            @pl.when(chunk == later * chunks_per_kv)
            def _(later=later):
                send_sums(later - 1)

        return carry

    lax.fori_loop(0, chunks, one_chunk, 0)
    send_sums(kv_heads - 1)

    for c in range(kv_heads):
        for slot, step in hops:
            @pl.when(has_later(step))
            def _(c=c, slot=slot, step=step):
                kv_copy(c, slot, step).wait_send()
                dkv_copy(c, slot, step).wait_recv()
                own[c] += recv[c, slot].astype(jnp.float32)
        gkv_ref[:, :, c * HEAD_DIM : (c + 1) * HEAD_DIM] = own[c].astype(jnp.bfloat16)
    for c in range(kv_heads):
        for slot, step in hops:
            @pl.when(has_earlier(step))
            def _(c=c, slot=slot, step=step):
                dkv_copy(c, slot, step).wait_send()
        for j in range(full):
            @pl.when(has_earlier(2 * j + 2))
            def _(c=c, j=j):
                pass_copy(c, j).wait_send()
                swap_copy(c, j).wait_send()

    def finish(chunk, carry):
        for step in range(1, n_t):
            g_copy(chunk, step).wait_send()
            dq_copy(chunk, step).wait()
        dq_own_copy(chunk).wait()
        return carry

    lax.fori_loop(0, chunks, finish, 0)


def hand_over(query_grad, key_grad):
    slice_rows, width = query_grad.shape
    parts = 8

    def move(a, b, a_out, b_out, a_held, b_held, in_sem, out_sem):
        ways = [(b, b_held, b_out)]
        for i in range(parts):
            part = (slice(None), pl.ds(i * (width // parts), width // parts))
            ways.append((a.at[part], a_held.at[part], a_out.at[part]))
        inward = [pltpu.make_async_copy(w[0], w[1], in_sem.at[i]) for i, w in enumerate(ways)]
        outward = [pltpu.make_async_copy(w[1], w[2], out_sem.at[i]) for i, w in enumerate(ways)]
        for copy in inward:
            copy.start()
        for first, second in zip(inward, outward):
            first.wait()
            second.start()
        for copy in outward:
            copy.wait()

    return pl.pallas_call(
        move,
        out_shape=(
            jax.ShapeDtypeStruct(query_grad.shape, query_grad.dtype),
            jax.ShapeDtypeStruct(key_grad.shape, key_grad.dtype),
        ),
        in_specs=[pl.BlockSpec(memory_space=pl.ANY)] * 2,
        out_specs=(pl.BlockSpec(memory_space=pl.ANY), pl.BlockSpec(memory_space=pl.ANY)),
        scratch_shapes=[
            pltpu.VMEM(query_grad.shape, query_grad.dtype),
            pltpu.VMEM(key_grad.shape, key_grad.dtype),
            pltpu.SemaphoreType.DMA((parts + 1,)),
            pltpu.SemaphoreType.DMA((parts + 1,)),
        ],
        compiler_params=pltpu.CompilerParams(vmem_limit_bytes=56 * 1024 * 1024),
    )(query_grad, key_grad)


def body(n_dp, n_t, queries, keys_values, grad_out, piece_lengths):
    rows, width = queries.shape
    kv_heads = keys_values.shape[2] // HEAD_DIM
    tokens = rows * n_dp
    group_rows = 36 * (tokens // 64)
    back = min(n_dp - 1, -(-(group_rows - 1) // rows) // 2 * 2 + 1)
    full = (back - 1) // 2
    keys = (back + 1) * rows
    chunks = width // (PAIR * HEAD_DIM)
    bf16, f32 = jnp.bfloat16, jnp.float32
    dma = pltpu.SemaphoreType.DMA
    lanes = PAIR * rows
    flops = 5 * 2 * rows * keys * width
    results = pl.pallas_call(
        functools.partial(kernel, n_dp, n_t, back),
        out_shape=(
            jax.ShapeDtypeStruct(grad_out.shape, bf16),
            jax.ShapeDtypeStruct(keys_values.shape, bf16),
        ),
        in_specs=[
            pl.BlockSpec(memory_space=pltpu.SMEM),
            pl.BlockSpec(memory_space=pl.ANY),
            pl.BlockSpec(memory_space=pl.ANY),
            pl.BlockSpec(memory_space=pl.ANY),
        ],
        out_specs=(pl.BlockSpec(memory_space=pl.ANY), pl.BlockSpec(memory_space=pltpu.VMEM)),
        scratch_shapes=[
            pltpu.VMEM((rows, width), bf16),
            pltpu.VMEM((rows, width), bf16),
            pltpu.VMEM((rows, width), bf16),
            pltpu.VMEM((kv_heads, 2, keys, HEAD_DIM), bf16),
            pltpu.VMEM((HEAD_DIM, keys), bf16),
            pltpu.VMEM((keys, rows), f32),
            pltpu.VMEM((keys, lanes), f32),
            pltpu.VMEM((keys, lanes), f32),
            pltpu.VMEM((keys, lanes), bf16),
            pltpu.VMEM((2, keys, HEAD_DIM), f32),
            pltpu.VMEM((kv_heads, 2, keys, HEAD_DIM), bf16),
            pltpu.VMEM((kv_heads, 2, rows, HEAD_DIM), f32),
            pltpu.VMEM((kv_heads, full + 2, 2, rows, HEAD_DIM), bf16),
            pltpu.VMEM((kv_heads, full, 2, rows, HEAD_DIM), bf16),
            dma(()),
            dma((kv_heads,)),
            dma(()),
            dma((chunks,)),
            dma((chunks, n_t - 1)),
            dma((chunks, n_t - 1)),
            dma((kv_heads, full + 2)),
            dma((kv_heads, full + 2)),
            dma((chunks, n_t - 1)),
            dma((chunks, n_t - 1)),
            dma((kv_heads, full + 2)),
            dma((kv_heads, full + 2)),
            dma((kv_heads, full)),
            dma((kv_heads, full)),
            dma((kv_heads, full)),
            dma((kv_heads, full)),
        ],
        compiler_params=pltpu.CompilerParams(
            collective_id=0, has_side_effects=True, vmem_limit_bytes=56 * 1024 * 1024
        ),
        cost_estimate=pl.CostEstimate(flops=flops, bytes_accessed=8 * rows * width, transcendentals=0),
    )(piece_lengths, queries, keys_values, grad_out)
    return hand_over(*results)


def solution(mesh):
    return jax.shard_map(
        functools.partial(body, mesh.shape["dp"], mesh.shape["tensor"]),
        mesh=mesh,
        in_specs=(P("dp", "tensor"), P(None, "dp", "tensor"), P(("dp", "tensor"), None), P()),
        out_specs=(P(("dp", "tensor"), None), P(None, "dp", "tensor")),
        check_vma=False,
    )
```

```python
import functools
import math

import jax
import jax.numpy as jnp
from jax import lax
from jax.experimental import pallas as pl
from jax.experimental.pallas import tpu as pltpu
from jax.sharding import PartitionSpec as P

HEAD_DIM = 128
GROUP = 8
PAIR = 4
MESH = pl.DeviceIdType.MESH
INV_ROOT = 1.0 / math.sqrt(HEAD_DIM)
EXP_SCALE = INV_ROOT * math.log2(math.e)


def dot(a, b):
    return jnp.dot(a, b, preferred_element_type=jnp.float32)


def dot_t(a, b):
    return lax.dot_general(a, b, (((1,), (1,)), ((), ())), preferred_element_type=jnp.float32)


def kernel(
    n_dp, n_t, back, len_ref, q_hbm, kv_hbm, go_hbm, gq_hbm, gkv_ref,
    q, g, dq, win, key_t, bias, prob, push, slope, acc, stage, own, recv, swap,
    q_sem, kv_own_sem, g_own_sem, dq_own_sem,
    g_send, g_recv, kv_send, kv_recv, dq_send, dq_recv, dkv_send, dkv_recv,
    pass_send, pass_recv, swap_send, swap_recv,
):
    d = lax.axis_index("dp")
    t = lax.axis_index("tensor")
    rows, width = q.shape
    kv_heads = win.shape[0]
    blocks = back + 1
    core = lax.rem(d, 2)
    partner = d + 1 - 2 * core
    full = (back - 1) // 2
    hops = [(j, 2 * j + 2) for j in range(full)] + [(full, 1), (full + 1, back)]

    def has_later(step):
        if step == 1:
            return core == 0
        return (d + step < n_dp) & ((core == 1) | (step % 2 == 0))

    def has_earlier(step):
        if step == 1:
            return core == 1
        return (d >= step) & ((core == 0) | (step % 2 == 0))
    slice_rows = go_hbm.shape[0]
    chunk_width = PAIR * HEAD_DIM
    chunks = width // chunk_width
    chunks_per_kv = GROUP // PAIR

    barrier = pltpu.get_barrier_semaphore()
    for step in range(1, n_dp):
        pl.semaphore_signal(barrier, inc=1, device_id=(lax.rem(d + step, n_dp), t), device_id_type=MESH)
    for step in range(1, n_t):
        pl.semaphore_signal(barrier, inc=1, device_id=(d, lax.rem(t + step, n_t)), device_id_type=MESH)

    def key_block(b):
        return pl.ds(b * rows, rows)

    q_copy = pltpu.make_async_copy(q_hbm, q, q_sem)
    q_copy.start()

    def kv_own_copy(c):
        return pltpu.make_async_copy(
            kv_hbm.at[:, :, pl.ds(c * HEAD_DIM, HEAD_DIM)],
            win.at[c, :, key_block(back), :],
            kv_own_sem.at[c],
        )

    for c in range(kv_heads):
        kv_own_copy(c).start()
    own_columns = pl.ds(pl.multiple_of(t * width, width), width)
    own_rows = pl.ds(pl.multiple_of(t * slice_rows, slice_rows), slice_rows)
    g_own_copy = pltpu.make_async_copy(go_hbm.at[:, own_columns], g.at[own_rows, :], g_own_sem)
    g_own_copy.start()

    pl.semaphore_wait(barrier, n_dp - 1 + n_t - 1)

    def dynamic_block(b):
        return pl.ds(pl.multiple_of(b * rows, rows), rows)

    def kv_copy(c, slot, step):
        return pltpu.make_async_remote_copy(
            src_ref=kv_hbm.at[:, :, pl.ds(c * HEAD_DIM, HEAD_DIM)],
            dst_ref=win.at[c, :, key_block(back - step), :],
            send_sem=kv_send.at[c, slot],
            recv_sem=kv_recv.at[c, slot],
            device_id=(lax.rem(d + step, n_dp), t),
            device_id_type=MESH,
        )

    def pass_copy(c, j):
        step = 2 * j + 2
        return pltpu.make_async_remote_copy(
            src_ref=win.at[c, :, key_block(back - step), :],
            dst_ref=win.at[c, :, dynamic_block(back - step - 1 + 2 * core), :],
            send_sem=pass_send.at[c, j],
            recv_sem=pass_recv.at[c, j],
            device_id=(partner, t),
            device_id_type=MESH,
        )

    def pass_arrival(c, j):
        step = 2 * j + 2
        return pltpu.make_async_remote_copy(
            src_ref=win.at[c, :, key_block(back - step), :],
            dst_ref=win.at[c, :, dynamic_block(back - step + 1 - 2 * core), :],
            send_sem=pass_send.at[c, j],
            recv_sem=pass_recv.at[c, j],
            device_id=(partner, t),
            device_id_type=MESH,
        )

    def pass_on(c):
        for j in range(full):
            @pl.when(has_earlier(2 * j + 2))
            def _(j=j):
                kv_copy(c, j, 2 * j + 2).wait_recv()
                pass_copy(c, j).start()

    def swap_copy(c, j):
        return pltpu.make_async_remote_copy(
            src_ref=stage.at[c, :, dynamic_block(back - 2 * j - 1 - 2 * core), :],
            dst_ref=swap.at[c, j],
            send_sem=swap_send.at[c, j],
            recv_sem=swap_recv.at[c, j],
            device_id=(partner, t),
            device_id_type=MESH,
        )

    def dkv_copy(c, slot, step):
        return pltpu.make_async_remote_copy(
            src_ref=stage.at[c, :, key_block(back - step), :],
            dst_ref=recv.at[c, slot],
            send_sem=dkv_send.at[c, slot],
            recv_sem=dkv_recv.at[c, slot],
            device_id=(lax.rem(d + n_dp - step, n_dp), t),
            device_id_type=MESH,
        )

    def send_sums(c):
        for j in range(full):
            @pl.when(has_earlier(2 * j + 2))
            def _(j=j):
                step = 2 * j + 2
                swap_copy(c, j).wait_recv()
                stage[c, :, key_block(back - step), :] = (
                    stage[c, :, key_block(back - step), :].astype(jnp.float32) + swap[c, j].astype(jnp.float32)
                ).astype(jnp.bfloat16)
                dkv_copy(c, j, step).start()

    def columns_of(holder, chunk):
        return pl.ds(pl.multiple_of(holder * width + chunk * chunk_width, chunk_width), chunk_width)

    def g_copy(chunk, step):
        target = lax.rem(t + step, n_t)
        return pltpu.make_async_remote_copy(
            src_ref=go_hbm.at[:, columns_of(target, chunk)],
            dst_ref=g.at[own_rows, columns_of(0, chunk)],
            send_sem=g_send.at[chunk, step - 1],
            recv_sem=g_recv.at[chunk, step - 1],
            device_id=(d, target),
            device_id_type=MESH,
        )

    def dq_copy(chunk, step):
        target = lax.rem(t + step, n_t)
        return pltpu.make_async_remote_copy(
            src_ref=dq.at[pl.ds(pl.multiple_of(target * slice_rows, slice_rows), slice_rows), columns_of(0, chunk)],
            dst_ref=gq_hbm.at[:, columns_of(t, chunk)],
            send_sem=dq_send.at[chunk, step - 1],
            recv_sem=dq_recv.at[chunk, step - 1],
            device_id=(d, target),
            device_id_type=MESH,
        )

    def dq_own_copy(chunk):
        return pltpu.make_async_copy(
            dq.at[own_rows, columns_of(0, chunk)], gq_hbm.at[:, columns_of(t, chunk)], dq_own_sem.at[chunk]
        )

    def send_kv(c):
        for slot, step in hops:
            @pl.when(has_later(step))
            def _(slot=slot, step=step):
                kv_copy(c, slot, step).start()

    send_kv(0)

    def send_g(chunk, carry):
        for step in range(1, n_t):
            g_copy(chunk, step).start()
        return carry

    lax.fori_loop(0, chunks, send_g, 0)
    for c in range(1, kv_heads):
        send_kv(c)

    for step in range(1, blocks):
        @pl.when(d < step)
        def _(step=step):
            win[:, :, key_block(back - step), :] = jnp.zeros((kv_heads, 2, rows, HEAD_DIM), jnp.bfloat16)

    pieces = len_ref.shape[0]
    ends = []
    total = jnp.int32(0)
    for piece in range(pieces):
        total = total + len_ref[piece]
        ends.append(total)
    query_ids = d * rows + lax.broadcasted_iota(jnp.int32, (8, rows), 1)
    query_piece = jnp.zeros((8, rows), jnp.int32)
    query_prompt = jnp.zeros((8, rows), jnp.int32)
    for piece in range(pieces):
        past = (query_ids >= ends[piece]).astype(jnp.int32)
        query_piece = query_piece + past
        if piece % 3 == 2:
            query_prompt = query_prompt + 3 * past
    query_ids, query_piece, query_prompt = query_ids[:1], query_piece[:1], query_prompt[:1]

    def mask_block(b, carry):
        key_ids = (d - back + b) * rows + lax.broadcasted_iota(jnp.int32, (rows, rows), 0)
        key_piece = jnp.zeros((rows, rows), jnp.int32)
        for piece in range(pieces):
            key_piece = key_piece + (key_ids >= ends[piece]).astype(jnp.int32)
        allowed = (key_ids <= query_ids) & (key_ids >= 0) & (
            (key_piece == query_piece) | (key_piece == query_prompt)
        )
        bias[pl.ds(pl.multiple_of(b * rows, rows), rows), :] = jnp.where(allowed, jnp.float32(0.0), jnp.float32(-1e30))
        return carry

    lax.fori_loop(0, blocks, mask_block, 0)
    q_copy.wait()
    g_own_copy.wait()
    pass_on(0)

    def one_chunk(chunk, carry):
        c = chunk // chunks_per_kv
        place = lax.rem(chunk, chunks_per_kv)

        @pl.when(place == 0)
        def _():
            pltpu.make_async_copy(
                kv_hbm.at[:, :, pl.ds(0, HEAD_DIM)], win.at[c, :, key_block(back), :], kv_own_sem.at[c]
            ).wait()
            for slot, step in hops[full:]:
                @pl.when(has_earlier(step))
                def _(slot=slot, step=step):
                    pltpu.make_async_remote_copy(
                        src_ref=kv_hbm.at[:, :, pl.ds(0, HEAD_DIM)],
                        dst_ref=win.at[c, :, key_block(back - step), :],
                        send_sem=kv_send.at[c, slot],
                        recv_sem=kv_recv.at[c, slot],
                        device_id=(lax.rem(d + step, n_dp), t),
                        device_id_type=MESH,
                    ).wait_recv()
            for j in range(full):
                @pl.when(has_earlier(2 * j + 2))
                def _(j=j):
                    pass_arrival(c, j).wait_recv()
            for b in range(blocks):
                key_t[:, key_block(b)] = win[c, 0, key_block(b), :].T
            acc[...] = jnp.zeros_like(acc)

        for step in range(1, n_t):
            g_copy(chunk, step).wait_recv()

        def heads_of(ref):
            return jnp.concatenate(
                [
                    ref[:, pl.ds(pl.multiple_of(chunk * chunk_width + u * HEAD_DIM, HEAD_DIM), HEAD_DIM)]
                    for u in range(PAIR)
                ],
                axis=0,
            )

        q_rows = heads_of(q)
        g_rows = heads_of(g)
        top = None
        for b in range(blocks):
            scores = dot_t(win[c, 0, key_block(b), :], q_rows)
            scores = scores + jnp.concatenate([bias[key_block(b), :]] * PAIR, axis=1)
            prob[key_block(b), :] = scores
            block_top = jnp.max(scores, axis=0, keepdims=True)
            top = block_top if top is None else jnp.maximum(top, block_top)
        weight_sum = jnp.zeros_like(top)
        push_sum = jnp.zeros_like(top)
        for b in range(blocks):
            weights = jnp.exp2((prob[key_block(b), :] - top) * EXP_SCALE)
            pushed = dot_t(win[c, 1, key_block(b), :], g_rows)
            prob[key_block(b), :] = weights
            push[key_block(b), :] = pushed
            weight_sum = weight_sum + jnp.sum(weights, axis=0, keepdims=True)
            push_sum = push_sum + jnp.sum(weights * pushed, axis=0, keepdims=True)
        inverse = 1.0 / weight_sum
        delta = push_sum * inverse
        for b in range(blocks):
            attend = prob[key_block(b), :] * inverse
            slopes = (attend * (push[key_block(b), :] - delta)).astype(jnp.bfloat16)
            slope[key_block(b), :] = slopes
            acc[0, key_block(b), :] += dot(slopes, q_rows)
            acc[1, key_block(b), :] += dot(attend.astype(jnp.bfloat16), g_rows)
        query_grad = dot(key_t[...], slope[...]) * INV_ROOT
        for u in range(PAIR):
            dq[:, pl.ds(pl.multiple_of(chunk * chunk_width + u * HEAD_DIM, HEAD_DIM), HEAD_DIM)] = (
                query_grad[:, u * rows : (u + 1) * rows].T.astype(jnp.bfloat16)
            )
        for step in range(1, n_t):
            dq_copy(chunk, step).start()
        dq_own_copy(chunk).start()

        @pl.when(place == chunks_per_kv - 1)
        def _():
            for b in range(blocks):
                key_part = acc[0, key_block(b), :] * INV_ROOT
                value_part = acc[1, key_block(b), :]
                if b == back:
                    own[c, 0] = key_part
                    own[c, 1] = value_part
                else:
                    stage[c, 0, key_block(b), :] = key_part.astype(jnp.bfloat16)
                    stage[c, 1, key_block(b), :] = value_part.astype(jnp.bfloat16)
            for j in range(full):
                @pl.when(has_earlier(2 * j + 2))
                def _(j=j):
                    swap_copy(c, j).start()
            for slot, step in hops[full:]:
                @pl.when(has_earlier(step))
                def _(slot=slot, step=step):
                    dkv_copy(c, slot, step).start()

        for later in range(1, kv_heads):
            @pl.when(chunk == (later - 1) * chunks_per_kv + 1)
            def _(later=later):
                pass_on(later)

            @pl.when(chunk == later * chunks_per_kv)
            def _(later=later):
                send_sums(later - 1)

        return carry

    lax.fori_loop(0, chunks, one_chunk, 0)
    send_sums(kv_heads - 1)

    for c in range(kv_heads):
        for slot, step in hops:
            @pl.when(has_later(step))
            def _(c=c, slot=slot, step=step):
                kv_copy(c, slot, step).wait_send()
                dkv_copy(c, slot, step).wait_recv()
                own[c] += recv[c, slot].astype(jnp.float32)
        gkv_ref[:, :, c * HEAD_DIM : (c + 1) * HEAD_DIM] = own[c].astype(jnp.bfloat16)
    for c in range(kv_heads):
        for slot, step in hops:
            @pl.when(has_earlier(step))
            def _(c=c, slot=slot, step=step):
                dkv_copy(c, slot, step).wait_send()
        for j in range(full):
            @pl.when(has_earlier(2 * j + 2))
            def _(c=c, j=j):
                pass_copy(c, j).wait_send()
                swap_copy(c, j).wait_send()

    def finish(chunk, carry):
        for step in range(1, n_t):
            g_copy(chunk, step).wait_send()
            dq_copy(chunk, step).wait()
        dq_own_copy(chunk).wait()
        return carry

    lax.fori_loop(0, chunks, finish, 0)


def hand_over(query_grad, key_grad):
    slice_rows, width = query_grad.shape
    parts = 8

    def move(a, b, a_out, b_out, a_held, b_held, in_sem, out_sem):
        ways = [(b, b_held, b_out)]
        for i in range(parts):
            part = (slice(None), pl.ds(i * (width // parts), width // parts))
            ways.append((a.at[part], a_held.at[part], a_out.at[part]))
        inward = [pltpu.make_async_copy(w[0], w[1], in_sem.at[i]) for i, w in enumerate(ways)]
        outward = [pltpu.make_async_copy(w[1], w[2], out_sem.at[i]) for i, w in enumerate(ways)]
        for copy in inward:
            copy.start()
        for first, second in zip(inward, outward):
            first.wait()
            second.start()
        for copy in outward:
            copy.wait()

    return pl.pallas_call(
        move,
        out_shape=(
            jax.ShapeDtypeStruct(query_grad.shape, query_grad.dtype),
            jax.ShapeDtypeStruct(key_grad.shape, key_grad.dtype),
        ),
        in_specs=[pl.BlockSpec(memory_space=pl.ANY)] * 2,
        out_specs=(pl.BlockSpec(memory_space=pl.ANY), pl.BlockSpec(memory_space=pl.ANY)),
        scratch_shapes=[
            pltpu.VMEM(query_grad.shape, query_grad.dtype),
            pltpu.VMEM(key_grad.shape, key_grad.dtype),
            pltpu.SemaphoreType.DMA((parts + 1,)),
            pltpu.SemaphoreType.DMA((parts + 1,)),
        ],
        compiler_params=pltpu.CompilerParams(vmem_limit_bytes=56 * 1024 * 1024),
    )(query_grad, key_grad)


def body(n_dp, n_t, queries, keys_values, grad_out, piece_lengths):
    rows, width = queries.shape
    kv_heads = keys_values.shape[2] // HEAD_DIM
    tokens = rows * n_dp
    group_rows = 36 * (tokens // 64)
    back = min(n_dp - 1, -(-(group_rows - 1) // rows) // 2 * 2 + 1)
    full = (back - 1) // 2
    keys = (back + 1) * rows
    chunks = width // (PAIR * HEAD_DIM)
    bf16, f32 = jnp.bfloat16, jnp.float32
    dma = pltpu.SemaphoreType.DMA
    lanes = PAIR * rows
    flops = 5 * 2 * rows * keys * width
    results = pl.pallas_call(
        functools.partial(kernel, n_dp, n_t, back),
        out_shape=(
            jax.ShapeDtypeStruct(grad_out.shape, bf16),
            jax.ShapeDtypeStruct(keys_values.shape, bf16),
        ),
        in_specs=[
            pl.BlockSpec(memory_space=pltpu.SMEM),
            pl.BlockSpec(memory_space=pl.ANY),
            pl.BlockSpec(memory_space=pl.ANY),
            pl.BlockSpec(memory_space=pl.ANY),
        ],
        out_specs=(pl.BlockSpec(memory_space=pl.ANY), pl.BlockSpec(memory_space=pltpu.VMEM)),
        scratch_shapes=[
            pltpu.VMEM((rows, width), bf16),
            pltpu.VMEM((rows, width), bf16),
            pltpu.VMEM((rows, width), bf16),
            pltpu.VMEM((kv_heads, 2, keys, HEAD_DIM), bf16),
            pltpu.VMEM((HEAD_DIM, keys), bf16),
            pltpu.VMEM((keys, rows), f32),
            pltpu.VMEM((keys, lanes), f32),
            pltpu.VMEM((keys, lanes), f32),
            pltpu.VMEM((keys, lanes), bf16),
            pltpu.VMEM((2, keys, HEAD_DIM), f32),
            pltpu.VMEM((kv_heads, 2, keys, HEAD_DIM), bf16),
            pltpu.VMEM((kv_heads, 2, rows, HEAD_DIM), f32),
            pltpu.VMEM((kv_heads, full + 2, 2, rows, HEAD_DIM), bf16),
            pltpu.VMEM((kv_heads, full, 2, rows, HEAD_DIM), bf16),
            dma(()),
            dma((kv_heads,)),
            dma(()),
            dma((chunks,)),
            dma((chunks, n_t - 1)),
            dma((chunks, n_t - 1)),
            dma((kv_heads, full + 2)),
            dma((kv_heads, full + 2)),
            dma((chunks, n_t - 1)),
            dma((chunks, n_t - 1)),
            dma((kv_heads, full + 2)),
            dma((kv_heads, full + 2)),
            dma((kv_heads, full)),
            dma((kv_heads, full)),
            dma((kv_heads, full)),
            dma((kv_heads, full)),
        ],
        compiler_params=pltpu.CompilerParams(
            collective_id=0, has_side_effects=True, vmem_limit_bytes=56 * 1024 * 1024
        ),
        cost_estimate=pl.CostEstimate(flops=flops, bytes_accessed=8 * rows * width, transcendentals=0),
    )(piece_lengths, queries, keys_values, grad_out)
    return hand_over(*results)


def solution(mesh):
    return jax.shard_map(
        functools.partial(body, mesh.shape["dp"], mesh.shape["tensor"]),
        mesh=mesh,
        in_specs=(P("dp", "tensor"), P(None, "dp", "tensor"), P(("dp", "tensor"), None), P()),
        out_specs=(P(("dp", "tensor"), None), P(None, "dp", "tensor")),
        check_vma=False,
    )
```
